512 devices in a mesh: inter: 16 (over z_lo, x, core), intra: 32 (over z_hi, y).
Axes of the slice: x: 4, y: 8, z: 8 (z_hi: 4, z_lo: 2; z = z_hi * 2 + z_lo), core: 2. Of those that a mesh axis runs over, the one named last changes fastest.
Arguments:
- hidden: bfloat16 [8192, 14336], P('intra', 'inter'), may hold values from -6 to 6
- cotangent: bfloat16 [8192, 4096], P('intra'), may hold values from -6 to 6
- packed_codes: int32 [3584, 4096], P('inter', 'intra'), may hold values from 0 to 65535
- block_scales: float32 [112, 32], P('inter', 'intra'), may hold values from 0.0006 to 0.006
Outputs:
- output: bfloat16 [8192, 4096], P(('intra', 'inter'))
- grad_hidden: bfloat16 [8192, 14336], P('intra', 'inter')
- grad_weight: float32 [14336, 4096], P('inter', 'intra')
The draws below stay inside these ranges and needn't reach their ends.
All inputs are finite; a program needn't handle non-finite values.
Results may differ from the reference program's by a relative error of at most 0.022.
Values may be sent and summed in bfloat16 or wider, within the bound.
No kernel may reach another device: no remote copies, remote signals or barrier semaphores. Data moves between devices by JAX's collectives and lax.ppermute only.
A program may use at most 128 MiB of HBM per device.

```python
import math
import jax
import jax.numpy as jnp
from jax import lax

D = 4096
FF = 14336
QB = 128
TOK_DEV = 256
TOKENS = 8192
N_INTER = 16
N_INTRA = 32


def touch_ends(result, rng, smallest, top_value):
    longest = result.shape.index(max(result.shape))
    spots = []
    for shift in (0, 1):
        where = [jax.random.randint(jax.random.fold_in(rng, axis), (), 0, length) for axis, length in enumerate(result.shape)]
        where[longest] = (where[longest] + shift) % result.shape[longest]
        spots.append(tuple(where))
    return result.at[spots[0]].set(smallest).at[spots[1]].set(top_value)


def block_levels(rng, extent, shards, smallest, largest):
    gain = 1.0
    for dim, shards_of in shards:
        heights = jax.random.uniform(jax.random.fold_in(jax.random.fold_in(rng, 6), dim), (shards_of,), jnp.float32, smallest / len(shards), largest / len(shards))
        gain = gain * jnp.repeat(jnp.exp(heights), extent[dim] // shards_of).reshape((-1,) + (1,) * (len(extent) - 1 - dim))
    return gain


def gaussian(stream_key, shape, deviation, reach, cuts=(), kind=jnp.bfloat16):
    drawn = jax.random.normal(stream_key, shape, jnp.float32) * deviation
    if len(cuts) > 0:
        drawn = block_levels(stream_key, shape, cuts, -0.22, 0.18) * drawn
    return jnp.clip(drawn, min=-reach, max=reach).astype(kind)


def setup_inputs(seed: int = 0) -> dict:
    keys = jax.random.split(jax.random.key(seed), 5)
    return {
        "hidden": gaussian(keys[0], (TOKENS, FF), 1.0, 6.0, ((0, 32), (1, 16))),
        "cotangent": gaussian(keys[1], (TOKENS, D), 1.0, 6.0, ((0, 32),)),
        "packed_codes": touch_ends(jax.random.randint(keys[2], (FF // 4, D), 0, 65536), jax.random.fold_in(keys[2], 1), 0, 65535).astype(jnp.int32),
        "block_scales": jnp.clip(jnp.exp(math.log(0.006) - 2.3025851 * jax.random.uniform(keys[3], (FF // QB, D // QB), jnp.float32) ** block_levels(keys[3], (FF // QB, D // QB), ((0, 16), (1, 32)), -0.2, 0.2)), 0.0006, 0.006),
    }


def unpack_weight(packed_codes, block_scales):
    layers = [jnp.bitwise_and(jnp.right_shift(packed_codes, 4 * nibble_slot), 15) - 8 for nibble_slot in range(4)]
    stacked = jnp.stack(layers, axis=1)
    unpacked = stacked.reshape(-1, packed_codes.shape[1]).astype(jnp.float32)
    row_total, col_total = unpacked.shape
    scale_rows, scale_cols = block_scales.shape
    blocked = unpacked.reshape(scale_rows, row_total // scale_rows, scale_cols, col_total // scale_cols)
    scaled = blocked * block_scales[:, None, :, None].astype(jnp.float32)
    return scaled.reshape(row_total, col_total).astype(jnp.bfloat16)


def reference(hidden, cotangent, packed_codes, block_scales):
    weight = unpack_weight(packed_codes, block_scales)
    width_dev = FF // N_INTER

    def add_group(total, group):
        start = (group * width_dev).astype(jnp.int32)
        hid_block = lax.dynamic_slice_in_dim(hidden, start, width_dev, 1)
        w_block = lax.dynamic_slice_in_dim(weight, start, width_dev, 0)
        partial_sum = jnp.dot(hid_block, w_block, preferred_element_type=jnp.float32).astype(jnp.bfloat16)
        return total + lax.optimization_barrier(partial_sum).astype(jnp.float32), None

    total_out, _ = lax.scan(add_group, jnp.zeros((TOKENS, D), jnp.float32), jnp.arange(N_INTER, dtype=jnp.int32))
    output = total_out.astype(jnp.bfloat16)
    grad_hidden = lax.dot_general(cotangent, weight, (((1,), (1,)), ((), ())), preferred_element_type=jnp.float32).astype(jnp.bfloat16)

    def add_tokens(total, group):
        start = (group * TOK_DEV).astype(jnp.int32)
        hid_rows = lax.dynamic_slice_in_dim(hidden, start, TOK_DEV, 0)
        cot_rows = lax.dynamic_slice_in_dim(cotangent, start, TOK_DEV, 0)
        grad_term = lax.dot_general(hid_rows, cot_rows, (((0,), (0,)), ((), ())), preferred_element_type=jnp.float32).astype(jnp.bfloat16)
        return total + lax.optimization_barrier(grad_term).astype(jnp.float32), None

    grad_weight, _ = lax.scan(add_tokens, jnp.zeros((FF, D), jnp.float32), jnp.arange(N_INTRA, dtype=jnp.int32))
    return output, grad_hidden, grad_weight
```

```python
import functools

import jax
import jax.numpy as jnp
from jax import lax
from jax.experimental import pallas as pl
from jax.experimental.pallas import tpu as pltpu
from jax.sharding import Mesh, PartitionSpec as P

Z_LO, X, CORE, Z_HI, Y = 2, 4, 2, 4, 8
FINE = ("z_lo", "x", "core", "z_hi", "y")
BF16, F32 = jnp.bfloat16, jnp.float32
HALF = 112
HIDDEN_DEV = 896
SCALE_ROWS = 8
EXACT = 2.0**34


def pack_block(codes, scales):
    words = jnp.bitwise_or(codes[:HALF], jnp.left_shift(codes[HALF:], 16))
    whole = (scales * EXACT).astype(jnp.int32)
    whole = jnp.pad(whole, ((0, SCALE_ROWS - whole.shape[0]), (0, 0)))
    whole = jnp.broadcast_to(whole, (SCALE_ROWS, codes.shape[1]))
    return jnp.concatenate([words, whole], axis=0)


def unpack_into(block, wide):
    words = block[:HALF]
    scales = block[HALF:].astype(F32) * (1.0 / EXACT)
    for slot in range(8):
        level = jnp.bitwise_and(jnp.right_shift(words, 4 * slot), 15) - 8
        wide[pl.ds((slot // 4) * 4 * HALF + slot % 4, HALF, stride=4), :] = level.astype(F32)
    parts = []
    for b in range(HIDDEN_DEV // 128):
        parts.append((wide[b * 128 : (b + 1) * 128, :] * scales[b : b + 1, :]).astype(BF16))
    return parts


def near_kernel(hid_ref, blocks_ref, out_ref, wide, weight):
    @pl.when(pl.program_id(0) == 0)
    def _():
        for z in range(Z_HI):
            for b, part in enumerate(unpack_into(blocks_ref[z], wide.at[z])):
                weight[b * 128 : (b + 1) * 128, z * 128 : (z + 1) * 128] = part

    out_ref[0] = jnp.dot(hid_ref[0], weight[...], preferred_element_type=F32).astype(BF16)


def near_product(hid, blocks):
    groups, rows, depth = hid.shape
    return pl.pallas_call(
        near_kernel,
        grid=(groups,),
        in_specs=[
            pl.BlockSpec((1, rows, depth), lambda g: (g, 0, 0)),
            pl.BlockSpec(blocks.shape, lambda g: (0, 0, 0)),
        ],
        out_specs=pl.BlockSpec((1, rows, Z_HI * 128), lambda g: (g, 0, 0)),
        out_shape=jax.ShapeDtypeStruct((groups, rows, Z_HI * 128), BF16),
        scratch_shapes=[
            pltpu.VMEM((Z_HI, HIDDEN_DEV, 128), F32),
            pltpu.VMEM((HIDDEN_DEV, Z_HI * 128), BF16),
        ],
        cost_estimate=pl.CostEstimate(
            flops=2 * groups * rows * depth * Z_HI * 128, bytes_accessed=8_000_000, transcendentals=0
        ),
        compiler_params=pltpu.CompilerParams(vmem_limit_bytes=32 * 1024 * 1024),
    )(hid, blocks)


def grad_hidden_kernel(cot_ref, blocks_ref, out_ref, wide, weight, total):
    step = pl.program_id(0)
    cot = []
    for z in range(Z_HI):
        for b, part in enumerate(unpack_into(blocks_ref[0, z], wide.at[z])):
            weight[b * 128 : (b + 1) * 128, z * 128 : (z + 1) * 128] = part
        cot.append(cot_ref[:, pl.ds(pl.multiple_of(z * Y * 128 + step * 128, 128), 128)])
    term = lax.dot_general(
        jnp.concatenate(cot, axis=1), weight[...], (((1,), (1,)), ((), ())), preferred_element_type=F32
    )

    @pl.when(step == 0)
    def _():
        total[...] = term

    @pl.when(step > 0)
    def _():
        total[...] += term

    @pl.when(step == pl.num_programs(0) - 1)
    def _():
        out_ref[...] = total[...].astype(BF16)


def grad_hidden_of(cot, blocks):
    rows = cot.shape[0]
    return pl.pallas_call(
        grad_hidden_kernel,
        grid=(Y,),
        in_specs=[
            pl.BlockSpec(cot.shape, lambda g: (0, 0)),
            pl.BlockSpec((1,) + blocks.shape[1:], lambda g: (g, 0, 0, 0)),
        ],
        out_specs=pl.BlockSpec((rows, HIDDEN_DEV), lambda g: (0, 0)),
        out_shape=jax.ShapeDtypeStruct((rows, HIDDEN_DEV), BF16),
        scratch_shapes=[
            pltpu.VMEM((Z_HI, HIDDEN_DEV, 128), F32),
            pltpu.VMEM((HIDDEN_DEV, Z_HI * 128), BF16),
            pltpu.VMEM((rows, HIDDEN_DEV), F32),
        ],
        cost_estimate=pl.CostEstimate(
            flops=2 * rows * HIDDEN_DEV * cot.shape[1], bytes_accessed=6_000_000, transcendentals=0
        ),
        compiler_params=pltpu.CompilerParams(vmem_limit_bytes=32 * 1024 * 1024),
    )(cot, blocks)


def ring(size, step):
    return [(i, (i + step) % size) for i in range(size)]


def per_device(hidden, cotangent, packed_codes, block_scales):
    tokens = hidden.shape[0]
    core = lax.axis_index("core")

    block = pack_block(packed_codes, block_scales)
    near = lax.all_gather(block, "z_hi")
    hid = lax.all_gather(hidden, "y")

    cols = cotangent.reshape(tokens, 2, 2, Y, 128)
    half = lax.dynamic_index_in_dim(cols, core, 1, keepdims=False)
    half = half.transpose(2, 0, 1, 3).reshape(Y, tokens, 256)
    mine = lax.all_to_all(half, "y", 0, 0)
    other = lax.ppermute(mine, "core", ring(CORE, 1))
    first = jnp.where(core == 0, mine, other)
    second = jnp.where(core == 0, other, mine)
    cot = jnp.concatenate([first, second], axis=2)

    term = lax.dot_general(hid, cot, (((0, 1), (0, 1)), ((), ())), preferred_element_type=F32).astype(BF16)
    terms = lax.all_to_all(term, "z_hi", split_axis=1, concat_axis=0, tiled=True)
    grad_weight = jnp.sum(terms.reshape(Z_HI, HIDDEN_DEV, 128).astype(F32), axis=0)

    partial = near_product(hid, near)
    partial = partial.reshape(Y, Z_LO * X, CORE, 16, 512)
    halves = lax.all_to_all(partial, "core", split_axis=2, concat_axis=2, tiled=True)
    pair = jnp.sum(halves.astype(F32), axis=2).astype(BF16)
    pieces = lax.all_to_all(pair, ("z_lo", "x"), split_axis=1, concat_axis=1, tiled=True)
    rows = jnp.sum(pieces.astype(F32), axis=1).astype(BF16)
    rows = lax.all_to_all(rows, "y", 0, 0)
    output = rows.reshape(Y, 16, Z_HI, 128).transpose(1, 2, 0, 3).reshape(16, Z_HI * Y * 128)

    every = lax.all_gather(near, "y")
    grad_hidden = grad_hidden_of(cotangent, every)
    return output, grad_hidden, grad_weight


def solution(mesh):
    fine = Mesh(mesh.devices.reshape(Z_LO, X, CORE, Z_HI, Y), FINE)
    inter, intra = ("z_lo", "x", "core"), ("z_hi", "y")
    return jax.shard_map(
        per_device,
        mesh=fine,
        in_specs=(P(intra, inter), P(intra, None), P(inter, intra), P(inter, intra)),
        out_specs=(P(intra + inter, None), P(intra, inter), P(inter, intra)),
        check_vma=False,
    )
```

```python
import functools

import jax
import jax.numpy as jnp
from jax import lax
from jax.experimental import pallas as pl
from jax.experimental.pallas import tpu as pltpu
from jax.sharding import Mesh, PartitionSpec as P

Z_LO, X, CORE, Z_HI, Y = 2, 4, 2, 4, 8
FINE = ("z_lo", "x", "core", "z_hi", "y")
BF16, F32 = jnp.bfloat16, jnp.float32
HALF = 112
HIDDEN_DEV = 896
SCALE_ROWS = 8
EXACT = 2.0**34
SIGNS = -0x77777778
VMEM_BYTES = 56 * 1024 * 1024


def pack_block(codes, scales):
    words = jnp.bitwise_or(codes[:HALF], jnp.left_shift(codes[HALF:], 16))
    words = jnp.bitwise_xor(words, SIGNS)
    whole = (scales * EXACT).astype(jnp.int32)
    whole = jnp.pad(whole, ((0, SCALE_ROWS - whole.shape[0]), (0, 0)))
    whole = jnp.broadcast_to(whole, (SCALE_ROWS, codes.shape[1]))
    return jnp.concatenate([words, whole], axis=0)


def level_of(words, slot):
    return jnp.right_shift(jnp.left_shift(words, 28 - 4 * slot), 28).astype(F32)


def scales_of(block):
    return block[HALF:].astype(F32) * (1.0 / EXACT)


def unpack_kernel(block_ref, out_ref, wide):
    block = block_ref[0]
    words, scales = block[:HALF], scales_of(block)
    for slot in range(8):
        wide[pl.ds((slot // 4) * 4 * HALF + slot % 4, HALF, stride=4), :] = level_of(words, slot)
    for b in range(HIDDEN_DEV // 128):
        rows = slice(b * 128, (b + 1) * 128)
        out_ref[rows, :] = (wide[rows, :] * scales[b : b + 1, :]).astype(BF16)


def near_weight(blocks):
    count, rows, lanes = blocks.shape
    return pl.pallas_call(
        unpack_kernel,
        grid=(count,),
        in_specs=[pl.BlockSpec((1, rows, lanes), lambda z: (z, 0, 0))],
        out_specs=pl.BlockSpec((HIDDEN_DEV, lanes), lambda z: (0, z)),
        out_shape=jax.ShapeDtypeStruct((HIDDEN_DEV, count * lanes), BF16),
        scratch_shapes=[pltpu.VMEM((HIDDEN_DEV, 128), F32)],
        cost_estimate=pl.CostEstimate(flops=2_000_000, bytes_accessed=1_200_000, transcendentals=0),
    )(blocks)


def assemble_kernel(place_ref, a_ref, b_ref, c_ref, out_ref):
    core, z_lo = place_ref[0], place_ref[1]
    for part, lo, co in (
        (a_ref, z_lo, core),
        (b_ref, 1 - z_lo, core),
        (c_ref.at[0], z_lo, 1 - core),
        (c_ref.at[1], 1 - z_lo, 1 - core),
    ):
        out_ref[:, pl.ds(pl.multiple_of((lo * 2 + co) * 64, 64), 64), :] = part[...]


def assemble(place, a, b, c):
    groups, quarter, width = a.shape
    step = 4
    part = pl.BlockSpec((step, quarter, width), lambda g, place: (g, 0, 0))
    return pl.pallas_call(
        assemble_kernel,
        grid_spec=pltpu.PrefetchScalarGridSpec(
            num_scalar_prefetch=1,
            grid=(groups // step,),
            in_specs=[part, part, pl.BlockSpec((2, step, quarter, width), lambda g, place: (0, g, 0, 0))],
            out_specs=pl.BlockSpec((step, 4 * quarter, width), lambda g, place: (g, 0, 0)),
        ),
        out_shape=jax.ShapeDtypeStruct((groups, 4 * quarter, width), BF16),
        cost_estimate=pl.CostEstimate(flops=0, bytes_accessed=4_000_000, transcendentals=0),
        compiler_params=pltpu.CompilerParams(vmem_limit_bytes=32 * 1024 * 1024),
    )(place, a, b, c)


def rows_kernel(other, place_ref, hid_ref, weight_ref, *rest):
    if other:
        out_ref, hid, weight, out, sems, out_sems = rest
        core = 1 - place_ref[0]
    else:
        got_ref, out_ref, hid, weight, out, sems, out_sems, got, got_sems = rest
        core = place_ref[0]
    chunks, groups, parts, rows, depth = hid.shape
    load = pltpu.make_async_copy(weight_ref, weight, sems.at[chunks])
    load.start()
    loads, adds, stores = [], [], []
    for i in range(chunks):
        at = pl.ds(i * groups, groups)
        loads.append(pltpu.make_async_copy(hid_ref.at[at, :, core], hid.at[i], sems.at[i]))
        loads[i].start()
        if not other:
            adds.append(pltpu.make_async_copy(got_ref.at[:, at], got.at[i], got_sems.at[i]))
            adds[i].start()
        stores.append(pltpu.make_async_copy(out.at[i], out_ref.at[:, at], out_sems.at[i]))
    load.wait()
    for i in range(chunks):
        loads[i].wait()
        product = jnp.dot(
            hid[i].reshape(groups * parts * rows, depth), weight[...], preferred_element_type=F32
        ).reshape(groups, parts, rows, weight.shape[1])
        if not other:
            adds[i].wait()
        for g in range(groups):
            value = product[g] if other else product[g] + got[i, :, g].astype(F32)
            out[i, :, g] = value.astype(BF16)
        stores[i].start()
    for store in stores:
        store.wait()


def core_rows(place, hid, weight, got=None):
    groups, chunks = hid.shape[0], 4
    step, depth = groups // chunks, hid.shape[2]
    parts, width = Z_LO * X, weight.shape[1]
    hid = hid.reshape(groups, parts, CORE, 16, depth)
    other = got is None
    args = (hid, weight) if other else (hid, weight, got)
    buffer = pltpu.VMEM((chunks, parts, step, 16, width), BF16)
    sems = pltpu.SemaphoreType.DMA((chunks,))
    return pl.pallas_call(
        functools.partial(rows_kernel, other),
        grid_spec=pltpu.PrefetchScalarGridSpec(
            num_scalar_prefetch=1,
            grid=(1,),
            in_specs=[pl.BlockSpec(memory_space=pl.ANY)] * len(args),
            out_specs=pl.BlockSpec(memory_space=pl.ANY),
            scratch_shapes=[
                pltpu.VMEM((chunks, step, parts, 16, depth), BF16),
                pltpu.VMEM(weight.shape, BF16),
                buffer,
                pltpu.SemaphoreType.DMA((chunks + 1,)),
                sems,
            ]
            + ([] if other else [buffer, sems]),
        ),
        out_shape=jax.ShapeDtypeStruct((parts, groups, 16, width), BF16),
        cost_estimate=pl.CostEstimate(
            flops=groups * 256 * HIDDEN_DEV * width, bytes_accessed=4_000_000, transcendentals=0
        ),
        compiler_params=pltpu.CompilerParams(vmem_limit_bytes=VMEM_BYTES),
    )(place, *args)


def row_widths(part):
    return ((0, 32), (1, 32), (2, 32), (3, 16)) if part == 0 else ((3, 16), (4, 32), (5, 32), (6, 32))


def grad_hidden_kernel(*refs):
    cot_refs, (blocks_ref, out_ref, weight, total, ordered) = refs[:Z_HI], refs[Z_HI:]
    step = pl.program_id(0)
    for z in range(Z_HI):
        block = blocks_ref[0, z]
        scales = scales_of(block)
        wide = [
            jnp.concatenate([jnp.broadcast_to(scales[b : b + 1], (rows, 128)) for b, rows in row_widths(part)], axis=0)
            for part in range(2)
        ]
        for slot in range(8):
            value = (level_of(block[:HALF], slot) * wide[slot // 4]).astype(BF16)
            weight[slot * HALF : (slot + 1) * HALF, z * 128 : (z + 1) * 128] = value
    cot = jnp.concatenate([ref[...] for ref in cot_refs], axis=1)
    term = lax.dot_general(weight[...], cot, (((1,), (1,)), ((), ())), preferred_element_type=F32)

    @pl.when(step == 0)
    def _():
        total[...] = term

    @pl.when(step > 0)
    def _():
        total[...] += term

    @pl.when(step == pl.num_programs(0) - 1)
    def _():
        for half in range(2):
            lanes = slice(half * 128, (half + 1) * 128)
            for slot in range(8):
                rows = pl.ds((slot // 4) * 4 * HALF + slot % 4, HALF, stride=4)
                ordered[half, rows, :] = total[slot * HALF : (slot + 1) * HALF, lanes]
            out_ref[lanes, :] = ordered[half].T.astype(BF16)


def grad_hidden_of(cot, blocks):
    rows = cot.shape[0]
    return pl.pallas_call(
        grad_hidden_kernel,
        grid=(Y,),
        in_specs=[pl.BlockSpec((rows, 128), functools.partial(lambda z, g: (0, z * Y + g), z)) for z in range(Z_HI)]
        + [pl.BlockSpec((1,) + blocks.shape[1:], lambda g: (g, 0, 0, 0))],
        out_specs=pl.BlockSpec((rows, HIDDEN_DEV), lambda g: (0, 0)),
        out_shape=jax.ShapeDtypeStruct((rows, HIDDEN_DEV), BF16),
        scratch_shapes=[
            pltpu.VMEM((HIDDEN_DEV, Z_HI * 128), BF16),
            pltpu.VMEM((HIDDEN_DEV, rows), F32),
            pltpu.VMEM((rows // 128, HIDDEN_DEV, 128), F32),
        ],
        cost_estimate=pl.CostEstimate(
            flops=2 * rows * HIDDEN_DEV * cot.shape[1], bytes_accessed=6_000_000, transcendentals=0
        ),
        compiler_params=pltpu.CompilerParams(vmem_limit_bytes=VMEM_BYTES),
    )(*([cot] * Z_HI), blocks)


def ring(size, step):
    return [(i, (i + step) % size) for i in range(size)]


def per_device(hidden, cotangent, packed_codes, block_scales):
    core, z_lo, z_hi = (lax.axis_index(name) for name in ("core", "z_lo", "z_hi"))
    place = jnp.stack([core, z_lo]).astype(jnp.int32)

    hid = lax.all_gather(hidden, "y")
    near = lax.all_gather(pack_block(packed_codes, block_scales), "z_hi")

    mine = lax.dynamic_slice_in_dim(cotangent, (z_lo * 2 + core) * 64, 64, axis=0).reshape(64, Z_HI, Y, 128)
    mine = lax.dynamic_slice_in_dim(jnp.concatenate([mine, mine], axis=1), z_hi, Z_HI, axis=1)
    mine = mine.transpose(2, 0, 1, 3).reshape(Y, 64, Z_HI * 128)
    a = lax.all_to_all(mine, "y", 0, 0)
    a, near = lax.optimization_barrier((a, near))
    b = lax.ppermute(a, "z_lo", ring(Z_LO, 1))
    weight = near_weight(near)
    c = lax.ppermute(jnp.stack([a, b]), "core", ring(CORE, 1))
    cot = assemble(place, a, b, c)

    hid, weight, cot = lax.optimization_barrier((hid, weight, cot))
    send = core_rows(place, hid, weight)
    got = lax.ppermute(send, "core", ring(CORE, 1))
    hid, cot, _ = lax.optimization_barrier((hid, cot, send))
    term = lax.dot_general(hid, cot, (((0, 1), (0, 1)), ((), ())), preferred_element_type=F32).astype(BF16)
    term = term.reshape(HIDDEN_DEV, Z_HI, 128).transpose(1, 0, 2)
    got, term = lax.optimization_barrier((got, term))
    pair = core_rows(place, hid, weight, got)
    pieces = lax.all_to_all(pair, ("z_lo", "x"), 0, 0)
    rows = jnp.sum(pieces.astype(F32), axis=0).astype(BF16)
    output = lax.all_to_all(rows, "y", 0, 0)
    output = output.reshape(Y, 16, Z_HI, 128).transpose(1, 2, 0, 3).reshape(16, Z_HI * Y * 128)

    term, pair = lax.optimization_barrier((term, pair))
    terms = [term[0]] + [lax.ppermute(term[d], "z_hi", ring(Z_HI, d)) for d in (1, 2, 3)]

    every = lax.all_gather(near, "y")
    every, rows = lax.optimization_barrier((every, rows))
    grad_hidden = grad_hidden_of(cotangent, every)
    grad_hidden, *terms = lax.optimization_barrier((grad_hidden, *terms))
    grad_weight = sum(each.astype(F32) for each in terms)
    return output, grad_hidden, grad_weight


def solution(mesh):
    fine = Mesh(mesh.devices.reshape(Z_LO, X, CORE, Z_HI, Y), FINE)
    inter, intra = ("z_lo", "x", "core"), ("z_hi", "y")
    return jax.shard_map(
        per_device,
        mesh=fine,
        in_specs=(P(intra, inter), P(intra, None), P(inter, intra), P(inter, intra)),
        out_specs=(P(intra + inter, None), P(intra, inter), P(inter, intra)),
        check_vma=False,
    )
```

```python
import functools

import jax
import jax.numpy as jnp
from jax import lax
from jax.experimental import pallas as pl
from jax.experimental.pallas import tpu as pltpu
from jax.sharding import Mesh, PartitionSpec as P

Z_LO, X, CORE, Z_HI, Y = 2, 4, 2, 4, 8
FINE = ("z_lo", "x", "core", "z_hi", "y")
BF16, F32 = jnp.bfloat16, jnp.float32
HALF = 112
HIDDEN_DEV = 896
SCALE_ROWS = 8
CHUNKS = 4
SHARE = 32
EXACT = 2.0**34
SIGNS = -0x77777778
VMEM_BYTES = 56 * 1024 * 1024


def pack_block(codes, scales):
    words = jnp.bitwise_or(codes[:HALF], jnp.left_shift(codes[HALF:], 16))
    words = jnp.bitwise_xor(words, SIGNS)
    whole = (scales * EXACT).astype(jnp.int32)
    whole = jnp.pad(whole, ((0, SCALE_ROWS - whole.shape[0]), (0, 0)))
    whole = jnp.broadcast_to(whole, (SCALE_ROWS, codes.shape[1]))
    return jnp.concatenate([words, whole], axis=0)


def level_of(words, slot):
    return jnp.right_shift(jnp.left_shift(words, 28 - 4 * slot), 28).astype(F32)


def scales_of(block):
    return block[HALF:].astype(F32) * (1.0 / EXACT)


def unpack_kernel(block_ref, out_ref, wide):
    block = block_ref[0]
    words, scales = block[:HALF], scales_of(block)
    for slot in range(8):
        wide[pl.ds((slot // 4) * 4 * HALF + slot % 4, HALF, stride=4), :] = level_of(words, slot)
    for b in range(HIDDEN_DEV // 128):
        rows = slice(b * 128, (b + 1) * 128)
        out_ref[rows, :] = (wide[rows, :] * scales[b : b + 1, :]).astype(BF16)


def near_weight(blocks):
    count, rows, lanes = blocks.shape
    return pl.pallas_call(
        unpack_kernel,
        grid=(count,),
        in_specs=[pl.BlockSpec((1, rows, lanes), lambda z: (z, 0, 0))],
        out_specs=pl.BlockSpec((HIDDEN_DEV, lanes), lambda z: (0, z)),
        out_shape=jax.ShapeDtypeStruct((HIDDEN_DEV, count * lanes), BF16),
        scratch_shapes=[pltpu.VMEM((HIDDEN_DEV, 128), F32)],
        cost_estimate=pl.CostEstimate(flops=2_000_000, bytes_accessed=1_200_000, transcendentals=0),
    )(blocks)


def assemble_kernel(place_ref, *refs):
    parts, other_ref, out_ref = refs[:4], refs[4], refs[5]
    core, z_lo, x_low, z_hi = place_ref[0], place_ref[1], place_ref[2], place_ref[3]
    order = [lax.rem(z_hi + d, Z_HI) for d in range(Z_HI)]
    for i in range(4):
        lo = z_lo if i % 2 == 0 else 1 - z_lo
        x = x_low if i // 2 == 0 else 1 - x_low
        for part, co in ((parts[i], core), (other_ref.at[i], 1 - core)):
            rows = pl.ds(pl.multiple_of(((lo * 2 + x) * 2 + co) * SHARE, SHARE), SHARE)
            for j, z in enumerate(order):
                out_ref[:, rows, j * 128 : (j + 1) * 128] = part[:, :, pl.ds(pl.multiple_of(z * 128, 128), 128)]


def assemble(place, parts, other):
    groups, share, width = parts[0].shape
    step = 4
    part = pl.BlockSpec((step, share, width), lambda g, place: (g, 0, 0))
    return pl.pallas_call(
        assemble_kernel,
        grid_spec=pltpu.PrefetchScalarGridSpec(
            num_scalar_prefetch=1,
            grid=(groups // step,),
            in_specs=[part] * 4 + [pl.BlockSpec((4, step, share, width), lambda g, place: (0, g, 0, 0))],
            out_specs=pl.BlockSpec((step, 8 * share, width), lambda g, place: (g, 0, 0)),
        ),
        out_shape=jax.ShapeDtypeStruct((groups, 8 * share, width), BF16),
        cost_estimate=pl.CostEstimate(flops=0, bytes_accessed=4_000_000, transcendentals=0),
        compiler_params=pltpu.CompilerParams(vmem_limit_bytes=32 * 1024 * 1024),
    )(place, *parts, other)


def products_kernel(
    place_ref, hid_ref, weight_ref, cot_ref, keep_ref, send_ref, own_ref, up_ref, far_ref, down_ref,
    hid, weight, cot, keep, send, sems, out_sems,
):
    core = place_ref[0]
    chunks = CHUNKS
    groups, rows, depth = hid.shape
    step, width = groups // chunks, weight.shape[1]
    load_weight = pltpu.make_async_copy(weight_ref, weight, sems.at[chunks])
    load_cot = pltpu.make_async_copy(cot_ref, cot, sems.at[chunks + 1])
    loads = [
        pltpu.make_async_copy(hid_ref.at[pl.ds(i * step, step)], hid.at[pl.ds(i * step, step)], sems.at[i])
        for i in range(chunks)
    ]
    load_weight.start()
    for load in loads:
        load.start()
    load_cot.start()
    load_weight.wait()
    for i in range(chunks):
        loads[i].wait()
        product = jnp.dot(
            hid[i * step : (i + 1) * step].reshape(step * rows, depth), weight[...], preferred_element_type=F32
        )
        product = product.astype(BF16).reshape(step, Z_LO * X, CORE, 16, width)
        for g in range(step):
            first, second = product[g, :, 0], product[g, :, 1]
            keep[:, i * step + g] = jnp.where(core == 0, first, second)
            send[:, i * step + g] = jnp.where(core == 0, second, first)
    stores = [
        pltpu.make_async_copy(send, send_ref, out_sems.at[0]),
        pltpu.make_async_copy(keep, keep_ref, out_sems.at[1]),
    ]
    for store in stores:
        store.start()
    load_cot.wait()
    tokens = hid[...].reshape(groups * rows, depth)
    columns = cot[...].reshape(groups * rows, width)

    def term(i):
        part = columns[:, i * 128 : (i + 1) * 128]
        return lax.dot_general(part, tokens, (((0,), (0,)), ((), ())), preferred_element_type=F32)

    for i, ref in enumerate((own_ref, up_ref, far_ref, down_ref)):
        ref[...] = term(i).astype(ref.dtype)
    for store in stores:
        store.wait()


def products(place, hid, weight, cot):
    groups, _, depth = hid.shape
    width = weight.shape[1]
    part = (Z_LO * X, groups, 16, width)
    anywhere, vmem = pl.BlockSpec(memory_space=pl.ANY), pl.BlockSpec(memory_space=pltpu.VMEM)
    return pl.pallas_call(
        products_kernel,
        grid_spec=pltpu.PrefetchScalarGridSpec(
            num_scalar_prefetch=1,
            grid=(1,),
            in_specs=[anywhere] * 3,
            out_specs=[anywhere] * 2 + [vmem] * 4,
            scratch_shapes=[
                pltpu.VMEM(hid.shape, BF16),
                pltpu.VMEM(weight.shape, BF16),
                pltpu.VMEM(cot.shape, BF16),
                pltpu.VMEM(part, BF16),
                pltpu.VMEM(part, BF16),
                pltpu.SemaphoreType.DMA((CHUNKS + 2,)),
                pltpu.SemaphoreType.DMA((2,)),
            ],
        ),
        out_shape=[jax.ShapeDtypeStruct(part, BF16)] * 2
        + [jax.ShapeDtypeStruct((128, depth), F32)]
        + [jax.ShapeDtypeStruct((128, depth), BF16)] * 3,
        cost_estimate=pl.CostEstimate(
            flops=4 * groups * 256 * depth * width, bytes_accessed=10_000_000, transcendentals=0
        ),
        compiler_params=pltpu.CompilerParams(vmem_limit_bytes=VMEM_BYTES),
    )(place, hid, weight, cot)


def row_widths(part):
    return ((0, 32), (1, 32), (2, 32), (3, 16)) if part == 0 else ((3, 16), (4, 32), (5, 32), (6, 32))


def grad_hidden_kernel(cot_ref, blocks_ref, out_ref, cot, blocks, even, odd, total, ordered, sems):
    step = Y // CHUNKS
    load_cot = pltpu.make_async_copy(cot_ref, cot, sems.at[CHUNKS])
    loads = [
        pltpu.make_async_copy(blocks_ref.at[pl.ds(i * step, step)], blocks.at[pl.ds(i * step, step)], sems.at[i])
        for i in range(CHUNKS)
    ]
    loads[0].start()
    load_cot.start()
    for load in loads[1:]:
        load.start()
    for y in range(Y):
        if y % step == 0:
            loads[y // step].wait()
        if y == 0:
            load_cot.wait()
        weight = odd if y % 2 else even
        for z in range(Z_HI):
            block = blocks[y, z]
            scales = scales_of(block)
            wide = [
                jnp.concatenate(
                    [jnp.broadcast_to(scales[b : b + 1], (rows, 128)) for b, rows in row_widths(part)], axis=0
                )
                for part in range(2)
            ]
            for slot in range(8):
                value = (level_of(block[:HALF], slot) * wide[slot // 4]).astype(BF16)
                weight[slot * HALF : (slot + 1) * HALF, z * 128 : (z + 1) * 128] = value
        columns = [cot[:, (z * Y + y) * 128 : (z * Y + y + 1) * 128] for z in range(Z_HI)]
        term = lax.dot_general(
            weight[...], jnp.concatenate(columns, axis=1), (((1,), (1,)), ((), ())), preferred_element_type=F32
        )
        if y == 0:
            total[...] = term
        else:
            total[...] += term
    for half in range(2):
        lanes = slice(half * 128, (half + 1) * 128)
        for slot in range(8):
            rows = pl.ds((slot // 4) * 4 * HALF + slot % 4, HALF, stride=4)
            ordered[half, rows, :] = total[slot * HALF : (slot + 1) * HALF, lanes]
        out_ref[lanes, :] = ordered[half].T.astype(BF16)


def grad_hidden_of(cot, blocks):
    rows = cot.shape[0]
    return pl.pallas_call(
        grad_hidden_kernel,
        in_specs=[pl.BlockSpec(memory_space=pl.ANY)] * 2,
        out_specs=pl.BlockSpec(memory_space=pltpu.VMEM),
        out_shape=jax.ShapeDtypeStruct((rows, HIDDEN_DEV), BF16),
        scratch_shapes=[
            pltpu.VMEM(cot.shape, BF16),
            pltpu.VMEM(blocks.shape, jnp.int32),
            pltpu.VMEM((HIDDEN_DEV, Z_HI * 128), BF16),
            pltpu.VMEM((HIDDEN_DEV, Z_HI * 128), BF16),
            pltpu.VMEM((HIDDEN_DEV, rows), F32),
            pltpu.VMEM((rows // 128, HIDDEN_DEV, 128), F32),
            pltpu.SemaphoreType.DMA((CHUNKS + 1,)),
        ],
        cost_estimate=pl.CostEstimate(
            flops=2 * rows * HIDDEN_DEV * cot.shape[1], bytes_accessed=6_000_000, transcendentals=0
        ),
        compiler_params=pltpu.CompilerParams(vmem_limit_bytes=VMEM_BYTES),
    )(cot, blocks)


def ring(size, step):
    return [(i, (i + step) % size) for i in range(size)]


def per_device(hidden, cotangent, packed_codes, block_scales):
    core, z_lo, x, z_hi = (lax.axis_index(name) for name in ("core", "z_lo", "x", "z_hi"))
    place = jnp.stack([core, z_lo, x % 2, z_hi]).astype(jnp.int32)

    hid = lax.all_gather(hidden, "y")
    near = lax.all_gather(pack_block(packed_codes, block_scales), "z_hi")

    first = ((z_lo * 2 + x % 2) * 2 + core) * SHARE
    mine = lax.dynamic_slice_in_dim(cotangent, first, SHARE, axis=0)
    mine = mine.reshape(SHARE, Z_HI, Y, 128).transpose(2, 0, 1, 3).reshape(Y, SHARE, Z_HI * 128)
    mine = lax.all_to_all(mine, "y", 0, 0)
    mine, near = lax.optimization_barrier((mine, near))
    parts = [mine]
    for flip_z, flip_x in ((1, 0), (0, 1), (1, 1)):
        pairs = [(z * X + i, (z ^ flip_z) * X + (i ^ flip_x)) for z in range(Z_LO) for i in range(X)]
        parts.append(lax.ppermute(mine, ("z_lo", "x"), pairs))
    weight = near_weight(near)
    other = lax.ppermute(jnp.stack(parts), "core", ring(CORE, 1))
    cot = assemble(place, parts, other)
    hid, weight, cot = lax.optimization_barrier((hid, weight, cot))
    keep, send, own, *others = products(place, hid, weight, cot)

    got = lax.ppermute(send, "core", ring(CORE, 1))
    pair = (keep.astype(F32) + got.astype(F32)).astype(BF16)

    pair, *others = lax.optimization_barrier((pair, *others))
    terms = [lax.ppermute(others[d - 1], "z_hi", ring(Z_HI, d)) for d in (2, 1, 3)]

    pieces = lax.all_to_all(pair, ("z_lo", "x"), 0, 0)
    rows = jnp.sum(pieces.astype(F32), axis=0).astype(BF16)
    output = lax.all_to_all(rows, "y", 0, 0)
    output = output.reshape(Y, 16, Z_HI, 128).transpose(1, 2, 0, 3).reshape(16, Z_HI * Y * 128)

    every = lax.all_gather(near, "y")
    every, rows = lax.optimization_barrier((every, rows))
    grad_hidden = grad_hidden_of(cotangent, every)
    grad_hidden, *terms = lax.optimization_barrier((grad_hidden, *terms))
    grad_weight = (own + sum(term.astype(F32) for term in terms)).T
    return output, grad_hidden, grad_weight


def solution(mesh):
    fine = Mesh(mesh.devices.reshape(Z_LO, X, CORE, Z_HI, Y), FINE)
    inter, intra = ("z_lo", "x", "core"), ("z_hi", "y")
    return jax.shard_map(
        per_device,
        mesh=fine,
        in_specs=(P(intra, inter), P(intra, None), P(inter, intra), P(inter, intra)),
        out_specs=(P(intra + inter, None), P(intra, inter), P(inter, intra)),
        check_vma=False,
    )
```

```python
import functools

import jax
import jax.numpy as jnp
from jax import lax
from jax.experimental import pallas as pl
from jax.experimental.pallas import tpu as pltpu
from jax.sharding import Mesh, PartitionSpec as P

Z_LO, X, CORE, Z_HI, Y = 2, 4, 2, 4, 8
FINE = ("z_lo", "x", "core", "z_hi", "y")
BF16, F32 = jnp.bfloat16, jnp.float32
HALF = 112
HIDDEN_DEV = 896
SCALE_ROWS = 8
CHUNKS = 4
HALVES = 4
SHARE = 32
EXACT = 2.0**34
SIGNS = -0x77777778
VMEM_BYTES = 56 * 1024 * 1024
VMEM_PRODUCTS = 50 * 1024 * 1024


def pack_block(codes, scales):
    words = jnp.bitwise_or(codes[:HALF], jnp.left_shift(codes[HALF:], 16))
    words = jnp.bitwise_xor(words, SIGNS)
    whole = (scales * EXACT).astype(jnp.int32)
    whole = jnp.pad(whole, ((0, SCALE_ROWS - whole.shape[0]), (0, 0)))
    whole = jnp.broadcast_to(whole, (SCALE_ROWS, codes.shape[1]))
    return jnp.concatenate([words, whole], axis=0)


def level_of(words, slot):
    return jnp.right_shift(jnp.left_shift(words, 28 - 4 * slot), 28).astype(F32)


def scales_of(block):
    return block[HALF:].astype(F32) * (1.0 / EXACT)


def unpack_kernel(block_ref, out_ref, wide):
    block = block_ref[0]
    words, scales = block[:HALF], scales_of(block)
    for slot in range(8):
        wide[pl.ds((slot // 4) * 4 * HALF + slot % 4, HALF, stride=4), :] = level_of(words, slot)
    for b in range(HIDDEN_DEV // 128):
        rows = slice(b * 128, (b + 1) * 128)
        out_ref[rows, :] = (wide[rows, :] * scales[b : b + 1, :]).astype(BF16)


def near_weight(blocks):
    count, rows, lanes = blocks.shape
    return pl.pallas_call(
        unpack_kernel,
        grid=(count,),
        in_specs=[pl.BlockSpec((1, rows, lanes), lambda z: (z, 0, 0))],
        out_specs=pl.BlockSpec((HIDDEN_DEV, lanes), lambda z: (0, z)),
        out_shape=jax.ShapeDtypeStruct((HIDDEN_DEV, count * lanes), BF16),
        scratch_shapes=[pltpu.VMEM((HIDDEN_DEV, 128), F32)],
        cost_estimate=pl.CostEstimate(flops=2_000_000, bytes_accessed=1_200_000, transcendentals=0),
    )(blocks)


def assemble_kernel(place_ref, *refs):
    parts, other_ref, out_ref = refs[:4], refs[4], refs[5]
    core, z_lo, x_low, z_hi = place_ref[0], place_ref[1], place_ref[2], place_ref[3]
    order = [lax.rem(z_hi + d, Z_HI) for d in range(Z_HI)]
    for i in range(4):
        lo = z_lo if i % 2 == 0 else 1 - z_lo
        x = x_low if i // 2 == 0 else 1 - x_low
        for part, co in ((parts[i], core), (other_ref.at[i], 1 - core)):
            rows = pl.ds(pl.multiple_of(((lo * 2 + x) * 2 + co) * SHARE, SHARE), SHARE)
            for j, z in enumerate(order):
                out_ref[:, rows, j * 128 : (j + 1) * 128] = part[:, :, pl.ds(pl.multiple_of(z * 128, 128), 128)]


def assemble(place, parts, other):
    groups, share, width = parts[0].shape
    step = 4
    part = pl.BlockSpec((step, share, width), lambda g, place: (g, 0, 0))
    return pl.pallas_call(
        assemble_kernel,
        grid_spec=pltpu.PrefetchScalarGridSpec(
            num_scalar_prefetch=1,
            grid=(groups // step,),
            in_specs=[part] * 4 + [pl.BlockSpec((4, step, share, width), lambda g, place: (0, g, 0, 0))],
            out_specs=pl.BlockSpec((step, 8 * share, width), lambda g, place: (g, 0, 0)),
        ),
        out_shape=jax.ShapeDtypeStruct((groups, 8 * share, width), BF16),
        cost_estimate=pl.CostEstimate(flops=0, bytes_accessed=4_000_000, transcendentals=0),
        compiler_params=pltpu.CompilerParams(vmem_limit_bytes=VMEM_BYTES),
    )(place, *parts, other)


def outputs_kernel(place_ref, hid_ref, weight_ref, keep_ref, send_ref, hid, weight, keep, send, sems, out_sems):
    core = place_ref[0]
    groups, rows, depth = hid.shape
    step, width = groups // CHUNKS, weight.shape[1]
    load_weight = pltpu.make_async_copy(weight_ref, weight, sems.at[CHUNKS])
    loads = [
        pltpu.make_async_copy(hid_ref.at[pl.ds(i * step, step)], hid.at[pl.ds(i * step, step)], sems.at[i])
        for i in range(CHUNKS)
    ]
    load_weight.start()
    for load in loads:
        load.start()
    load_weight.wait()
    stores = []
    for i in range(CHUNKS):
        loads[i].wait()
        product = jnp.dot(
            hid[i * step : (i + 1) * step].reshape(step * rows, depth), weight[...], preferred_element_type=F32
        )
        product = product.astype(BF16).reshape(step, Z_LO * X, CORE, 16, width)
        for g in range(step):
            first, second = product[g, :, 0], product[g, :, 1]
            keep[:, i * step + g] = jnp.where(core == 0, first, second)
            send[:, i * step + g] = jnp.where(core == 0, second, first)
        at = pl.ds(i * step, step)
        stores.append(pltpu.make_async_copy(send.at[:, at], send_ref.at[:, at], out_sems.at[0, i]))
        stores.append(pltpu.make_async_copy(keep.at[:, at], keep_ref.at[:, at], out_sems.at[1, i]))
        for store in stores[-2:]:
            store.start()
    for store in stores:
        store.wait()


def ring_outputs(place, hid, weight):
    groups, _, depth = hid.shape
    width = weight.shape[1]
    part = (Z_LO * X, groups, 16, width)
    anywhere = pl.BlockSpec(memory_space=pl.ANY)
    return pl.pallas_call(
        outputs_kernel,
        grid_spec=pltpu.PrefetchScalarGridSpec(
            num_scalar_prefetch=1,
            grid=(1,),
            in_specs=[anywhere] * 2,
            out_specs=[anywhere] * 2,
            scratch_shapes=[
                pltpu.VMEM(hid.shape, BF16),
                pltpu.VMEM(weight.shape, BF16),
                pltpu.VMEM(part, BF16),
                pltpu.VMEM(part, BF16),
                pltpu.SemaphoreType.DMA((CHUNKS + 1,)),
                pltpu.SemaphoreType.DMA((2, CHUNKS)),
            ],
        ),
        out_shape=[jax.ShapeDtypeStruct(part, BF16)] * 2,
        cost_estimate=pl.CostEstimate(
            flops=2 * groups * 256 * depth * width, bytes_accessed=7_000_000, transcendentals=0
        ),
        compiler_params=pltpu.CompilerParams(vmem_limit_bytes=VMEM_PRODUCTS),
    )(place, hid, weight)


def terms_kernel(hid_ref, cot_ref, own_ref, up_ref, far_ref, down_ref, hid, cot, sems):
    groups, rows, depth = hid.shape
    step, width = groups // HALVES, cot.shape[2]
    loads = []
    for i in range(HALVES):
        at = pl.ds(i * step, step)
        loads.append(pltpu.make_async_copy(cot_ref.at[at], cot.at[at], sems.at[0, i]))
        loads.append(pltpu.make_async_copy(hid_ref.at[at], hid.at[at], sems.at[1, i]))
    for load in loads:
        load.start()
    total = None
    for i in range(HALVES):
        loads[2 * i].wait()
        loads[2 * i + 1].wait()
        part = slice(i * step, (i + 1) * step)
        term = lax.dot_general(
            cot[part].reshape(step * rows, width),
            hid[part].reshape(step * rows, depth),
            (((0,), (0,)), ((), ())),
            preferred_element_type=F32,
        )
        total = term if total is None else total + term
    for i, ref in enumerate((own_ref, up_ref, far_ref, down_ref)):
        ref[...] = total[i * 128 : (i + 1) * 128].astype(BF16)


def gradient_terms(hid, cot):
    groups, rows, depth = hid.shape
    width = cot.shape[2]
    return pl.pallas_call(
        terms_kernel,
        in_specs=[pl.BlockSpec(memory_space=pl.ANY)] * 2,
        out_specs=[pl.BlockSpec(memory_space=pltpu.VMEM)] * 4,
        scratch_shapes=[
            pltpu.VMEM(hid.shape, BF16),
            pltpu.VMEM(cot.shape, BF16),
            pltpu.SemaphoreType.DMA((2, HALVES)),
        ],
        out_shape=[jax.ShapeDtypeStruct((128, depth), BF16)] * 4,
        cost_estimate=pl.CostEstimate(
            flops=2 * groups * rows * depth * width, bytes_accessed=7_000_000, transcendentals=0
        ),
        compiler_params=pltpu.CompilerParams(vmem_limit_bytes=VMEM_PRODUCTS),
    )(hid, cot)


def row_widths(part):
    return ((0, 32), (1, 32), (2, 32), (3, 16)) if part == 0 else ((3, 16), (4, 32), (5, 32), (6, 32))


def grad_hidden_kernel(cot_ref, blocks_ref, out_ref, cot, blocks, even, odd, total, ordered, sems):
    step = Y // CHUNKS
    load_cot = pltpu.make_async_copy(cot_ref, cot, sems.at[CHUNKS])
    loads = [
        pltpu.make_async_copy(blocks_ref.at[pl.ds(i * step, step)], blocks.at[pl.ds(i * step, step)], sems.at[i])
        for i in range(CHUNKS)
    ]
    loads[0].start()
    load_cot.start()
    for load in loads[1:]:
        load.start()
    for y in range(Y):
        if y % step == 0:
            loads[y // step].wait()
        if y == 0:
            load_cot.wait()
        weight = odd if y % 2 else even
        for z in range(Z_HI):
            block = blocks[y, z]
            scales = scales_of(block)
            wide = [
                jnp.concatenate(
                    [jnp.broadcast_to(scales[b : b + 1], (rows, 128)) for b, rows in row_widths(part)], axis=0
                )
                for part in range(2)
            ]
            for slot in range(8):
                value = (level_of(block[:HALF], slot) * wide[slot // 4]).astype(BF16)
                weight[slot * HALF : (slot + 1) * HALF, z * 128 : (z + 1) * 128] = value
        columns = [cot[:, (z * Y + y) * 128 : (z * Y + y + 1) * 128] for z in range(Z_HI)]
        term = lax.dot_general(
            weight[...], jnp.concatenate(columns, axis=1), (((1,), (1,)), ((), ())), preferred_element_type=F32
        )
        if y == 0:
            total[...] = term
        else:
            total[...] += term
    for half in range(2):
        lanes = slice(half * 128, (half + 1) * 128)
        for slot in range(8):
            rows = pl.ds((slot // 4) * 4 * HALF + slot % 4, HALF, stride=4)
            ordered[half, rows, :] = total[slot * HALF : (slot + 1) * HALF, lanes]
        out_ref[lanes, :] = ordered[half].T.astype(BF16)


def grad_hidden_of(cot, blocks):
    rows = cot.shape[0]
    return pl.pallas_call(
        grad_hidden_kernel,
        in_specs=[pl.BlockSpec(memory_space=pl.ANY)] * 2,
        out_specs=pl.BlockSpec(memory_space=pltpu.VMEM),
        out_shape=jax.ShapeDtypeStruct((rows, HIDDEN_DEV), BF16),
        scratch_shapes=[
            pltpu.VMEM(cot.shape, BF16),
            pltpu.VMEM(blocks.shape, jnp.int32),
            pltpu.VMEM((HIDDEN_DEV, Z_HI * 128), BF16),
            pltpu.VMEM((HIDDEN_DEV, Z_HI * 128), BF16),
            pltpu.VMEM((HIDDEN_DEV, rows), F32),
            pltpu.VMEM((rows // 128, HIDDEN_DEV, 128), F32),
            pltpu.SemaphoreType.DMA((CHUNKS + 1,)),
        ],
        cost_estimate=pl.CostEstimate(
            flops=2 * rows * HIDDEN_DEV * cot.shape[1], bytes_accessed=6_000_000, transcendentals=0
        ),
        compiler_params=pltpu.CompilerParams(vmem_limit_bytes=VMEM_BYTES),
    )(cot, blocks)


def ring(size, step):
    return [(i, (i + step) % size) for i in range(size)]


def per_device(hidden, cotangent, packed_codes, block_scales):
    core, z_lo, x, z_hi = (lax.axis_index(name) for name in ("core", "z_lo", "x", "z_hi"))
    place = jnp.stack([core, z_lo, x % 2, z_hi]).astype(jnp.int32)

    hid = lax.all_gather(hidden, "y")
    near = lax.all_gather(pack_block(packed_codes, block_scales), "z_hi")

    first = ((z_lo * 2 + x % 2) * 2 + core) * SHARE
    mine = lax.dynamic_slice_in_dim(cotangent, first, SHARE, axis=0)
    mine = mine.reshape(SHARE, Z_HI, Y, 128).transpose(2, 0, 1, 3).reshape(Y, SHARE, Z_HI * 128)
    mine = lax.all_to_all(mine, "y", 0, 0)
    mine, near = lax.optimization_barrier((mine, near))
    parts = [mine]
    for flip_z, flip_x in ((1, 0), (0, 1), (1, 1)):
        pairs = [(z * X + i, (z ^ flip_z) * X + (i ^ flip_x)) for z in range(Z_LO) for i in range(X)]
        parts.append(lax.ppermute(mine, ("z_lo", "x"), pairs))
    weight = near_weight(near)
    other = lax.ppermute(jnp.stack(parts), "core", ring(CORE, 1))
    cot = assemble(place, parts, other)
    hid, weight, cot = lax.optimization_barrier((hid, weight, cot))
    keep, send = ring_outputs(place, hid, weight)

    got = lax.ppermute(send, "core", ring(CORE, 1))
    hid, cot, send = lax.optimization_barrier((hid, cot, send))
    own, *others = gradient_terms(hid, cot)
    got, own, *others = lax.optimization_barrier((got, own, *others))
    pair = (keep.astype(F32) + got.astype(F32)).astype(BF16)

    pair, *others = lax.optimization_barrier((pair, *others))
    terms = [lax.ppermute(others[d - 1], "z_hi", ring(Z_HI, d)) for d in (2, 1, 3)]

    pieces = lax.all_to_all(pair, ("z_lo", "x"), 0, 0)
    rows = jnp.sum(pieces.astype(F32), axis=0).astype(BF16)
    output = lax.all_to_all(rows, "y", 0, 0)
    output = output.reshape(Y, 16, Z_HI, 128).transpose(1, 2, 0, 3).reshape(16, Z_HI * Y * 128)

    every = lax.all_gather(near, "y")
    every, rows = lax.optimization_barrier((every, rows))
    grad_hidden = grad_hidden_of(cotangent, every)
    grad_hidden, *terms = lax.optimization_barrier((grad_hidden, *terms))
    grad_weight = sum(term.astype(F32) for term in (own, *terms)).T
    return output, grad_hidden, grad_weight


def solution(mesh):
    fine = Mesh(mesh.devices.reshape(Z_LO, X, CORE, Z_HI, Y), FINE)
    inter, intra = ("z_lo", "x", "core"), ("z_hi", "y")
    return jax.shard_map(
        per_device,
        mesh=fine,
        in_specs=(P(intra, inter), P(intra, None), P(inter, intra), P(inter, intra)),
        out_specs=(P(intra + inter, None), P(intra, inter), P(inter, intra)),
        check_vma=False,
    )
```

```python
import functools

import jax
import jax.numpy as jnp
from jax import lax
from jax.experimental import pallas as pl
from jax.experimental.pallas import tpu as pltpu
from jax.sharding import Mesh, PartitionSpec as P

Z_LO, X, CORE, Z_HI, Y = 2, 4, 2, 4, 8
FINE = ("z_lo", "x", "core", "z_hi", "y")
BF16, F32 = jnp.bfloat16, jnp.float32
HALF = 112
HIDDEN_DEV = 896
SCALE_ROWS = 8
CHUNKS = 4
HALVES = 4
SHARE = 32
EXACT = 2.0**34
SIGNS = -0x77777778
VMEM_BYTES = 56 * 1024 * 1024
VMEM_PRODUCTS = 50 * 1024 * 1024


def pack_block(codes, scales):
    words = jnp.bitwise_or(codes[:HALF], jnp.left_shift(codes[HALF:], 16))
    words = jnp.bitwise_xor(words, SIGNS)
    whole = (scales * EXACT).astype(jnp.int32)
    whole = jnp.pad(whole, ((0, SCALE_ROWS - whole.shape[0]), (0, 0)))
    whole = jnp.broadcast_to(whole, (SCALE_ROWS, codes.shape[1]))
    return jnp.concatenate([words, whole], axis=0)


def level_of(words, slot):
    return jnp.right_shift(jnp.left_shift(words, 28 - 4 * slot), 28).astype(F32)


def scales_of(block):
    return block[HALF:].astype(F32) * (1.0 / EXACT)


def unpack_kernel(block_ref, out_ref, wide):
    block = block_ref[0]
    words, scales = block[:HALF], scales_of(block)
    for slot in range(8):
        wide[pl.ds((slot // 4) * 4 * HALF + slot % 4, HALF, stride=4), :] = level_of(words, slot)
    for b in range(HIDDEN_DEV // 128):
        rows = slice(b * 128, (b + 1) * 128)
        out_ref[rows, :] = (wide[rows, :] * scales[b : b + 1, :]).astype(BF16)


def near_weight(blocks):
    count, rows, lanes = blocks.shape
    return pl.pallas_call(
        unpack_kernel,
        grid=(count,),
        in_specs=[pl.BlockSpec((1, rows, lanes), lambda z: (z, 0, 0))],
        out_specs=pl.BlockSpec((HIDDEN_DEV, lanes), lambda z: (0, z)),
        out_shape=jax.ShapeDtypeStruct((HIDDEN_DEV, count * lanes), BF16),
        scratch_shapes=[pltpu.VMEM((HIDDEN_DEV, 128), F32)],
        cost_estimate=pl.CostEstimate(flops=2_000_000, bytes_accessed=1_200_000, transcendentals=0),
    )(blocks)


def assemble_kernel(place_ref, *refs):
    parts, other_ref, out_ref = refs[:4], refs[4], refs[5]
    core, z_lo, x_low, z_hi = place_ref[0], place_ref[1], place_ref[2], place_ref[3]
    order = [lax.rem(z_hi + d, Z_HI) for d in range(Z_HI)]
    for i in range(4):
        lo = z_lo if i % 2 == 0 else 1 - z_lo
        x = x_low if i // 2 == 0 else 1 - x_low
        for part, co in ((parts[i], core), (other_ref.at[i], 1 - core)):
            rows = pl.ds(pl.multiple_of(((lo * 2 + x) * 2 + co) * SHARE, SHARE), SHARE)
            for j, z in enumerate(order):
                out_ref[:, rows, j * 128 : (j + 1) * 128] = part[:, :, pl.ds(pl.multiple_of(z * 128, 128), 128)]


def assemble(place, parts, other):
    groups, share, width = parts[0].shape
    step = 4
    part = pl.BlockSpec((step, share, width), lambda g, place: (g, 0, 0))
    return pl.pallas_call(
        assemble_kernel,
        grid_spec=pltpu.PrefetchScalarGridSpec(
            num_scalar_prefetch=1,
            grid=(groups // step,),
            in_specs=[part] * 4 + [pl.BlockSpec((4, step, share, width), lambda g, place: (0, g, 0, 0))],
            out_specs=pl.BlockSpec((step, 8 * share, width), lambda g, place: (g, 0, 0)),
        ),
        out_shape=jax.ShapeDtypeStruct((groups, 8 * share, width), BF16),
        cost_estimate=pl.CostEstimate(flops=0, bytes_accessed=4_000_000, transcendentals=0),
        compiler_params=pltpu.CompilerParams(vmem_limit_bytes=VMEM_BYTES),
    )(place, *parts, other)


def outputs_kernel(place_ref, hid_ref, weight_ref, keep_ref, send_ref, hid, weight, keep, send, sems, out_sems):
    core = place_ref[0]
    groups, rows, depth = hid.shape
    step, width = groups // CHUNKS, weight.shape[1]
    load_weight = pltpu.make_async_copy(weight_ref, weight, sems.at[CHUNKS])
    loads = [
        pltpu.make_async_copy(hid_ref.at[pl.ds(i * step, step)], hid.at[pl.ds(i * step, step)], sems.at[i])
        for i in range(CHUNKS)
    ]
    load_weight.start()
    for load in loads:
        load.start()
    load_weight.wait()
    stores = []
    for i in range(CHUNKS):
        loads[i].wait()
        product = jnp.dot(
            hid[i * step : (i + 1) * step].reshape(step * rows, depth), weight[...], preferred_element_type=F32
        )
        product = product.astype(BF16).reshape(step, Z_LO * X, CORE, 16, width)
        for g in range(step):
            first, second = product[g, :, 0], product[g, :, 1]
            keep[:, i * step + g] = jnp.where(core == 0, first, second)
            send[:, i * step + g] = jnp.where(core == 0, second, first)
        at = pl.ds(i * step, step)
        stores.append(pltpu.make_async_copy(send.at[:, at], send_ref.at[:, at], out_sems.at[0, i]))
        stores.append(pltpu.make_async_copy(keep.at[:, at], keep_ref.at[:, at], out_sems.at[1, i]))
        for store in stores[-2:]:
            store.start()
    for store in stores:
        store.wait()


def ring_outputs(place, hid, weight):
    groups, _, depth = hid.shape
    width = weight.shape[1]
    part = (Z_LO * X, groups, 16, width)
    anywhere = pl.BlockSpec(memory_space=pl.ANY)
    return pl.pallas_call(
        outputs_kernel,
        grid_spec=pltpu.PrefetchScalarGridSpec(
            num_scalar_prefetch=1,
            grid=(1,),
            in_specs=[anywhere] * 2,
            out_specs=[anywhere] * 2,
            scratch_shapes=[
                pltpu.VMEM(hid.shape, BF16),
                pltpu.VMEM(weight.shape, BF16),
                pltpu.VMEM(part, BF16),
                pltpu.VMEM(part, BF16),
                pltpu.SemaphoreType.DMA((CHUNKS + 1,)),
                pltpu.SemaphoreType.DMA((2, CHUNKS)),
            ],
        ),
        out_shape=[jax.ShapeDtypeStruct(part, BF16)] * 2,
        cost_estimate=pl.CostEstimate(
            flops=2 * groups * 256 * depth * width, bytes_accessed=7_000_000, transcendentals=0
        ),
        compiler_params=pltpu.CompilerParams(vmem_limit_bytes=VMEM_PRODUCTS),
    )(place, hid, weight)


def terms_kernel(hid_ref, cot_ref, own_ref, up_ref, far_ref, down_ref, hid, cot, sems):
    groups, rows, depth = hid.shape
    step, width = groups // HALVES, cot.shape[2]
    loads = []
    for i in range(HALVES):
        at = pl.ds(i * step, step)
        loads.append(pltpu.make_async_copy(cot_ref.at[at], cot.at[at], sems.at[0, i]))
        loads.append(pltpu.make_async_copy(hid_ref.at[at], hid.at[at], sems.at[1, i]))
    for load in loads:
        load.start()
    total = None
    for i in range(HALVES):
        loads[2 * i].wait()
        loads[2 * i + 1].wait()
        part = slice(i * step, (i + 1) * step)
        term = lax.dot_general(
            cot[part].reshape(step * rows, width),
            hid[part].reshape(step * rows, depth),
            (((0,), (0,)), ((), ())),
            preferred_element_type=F32,
        )
        total = term if total is None else total + term
    for i, ref in enumerate((own_ref, up_ref, far_ref, down_ref)):
        ref[...] = total[i * 128 : (i + 1) * 128].astype(BF16)


def gradient_terms(hid, cot):
    groups, rows, depth = hid.shape
    width = cot.shape[2]
    return pl.pallas_call(
        terms_kernel,
        in_specs=[pl.BlockSpec(memory_space=pl.ANY)] * 2,
        out_specs=[pl.BlockSpec(memory_space=pltpu.VMEM)] * 4,
        scratch_shapes=[
            pltpu.VMEM(hid.shape, BF16),
            pltpu.VMEM(cot.shape, BF16),
            pltpu.SemaphoreType.DMA((2, HALVES)),
        ],
        out_shape=[jax.ShapeDtypeStruct((128, depth), BF16)] * 4,
        cost_estimate=pl.CostEstimate(
            flops=2 * groups * rows * depth * width, bytes_accessed=7_000_000, transcendentals=0
        ),
        compiler_params=pltpu.CompilerParams(vmem_limit_bytes=VMEM_PRODUCTS),
    )(hid, cot)


def row_widths(part):
    return ((0, 32), (1, 32), (2, 32), (3, 16)) if part == 0 else ((3, 16), (4, 32), (5, 32), (6, 32))


def grad_hidden_kernel(cot_ref, blocks_ref, out_ref, cot, blocks, even, odd, total, ordered, sems):
    step = Y // CHUNKS
    load_cot = pltpu.make_async_copy(cot_ref, cot, sems.at[CHUNKS])
    loads = [
        pltpu.make_async_copy(blocks_ref.at[pl.ds(i * step, step)], blocks.at[pl.ds(i * step, step)], sems.at[i])
        for i in range(CHUNKS)
    ]
    loads[0].start()
    load_cot.start()
    for load in loads[1:]:
        load.start()
    for y in range(Y):
        if y % step == 0:
            loads[y // step].wait()
        if y == 0:
            load_cot.wait()
        weight = odd if y % 2 else even
        for z in range(Z_HI):
            block = blocks[y, z]
            scales = scales_of(block)
            wide = [
                jnp.concatenate(
                    [jnp.broadcast_to(scales[b : b + 1], (rows, 128)) for b, rows in row_widths(part)], axis=0
                )
                for part in range(2)
            ]
            for slot in range(8):
                value = (level_of(block[:HALF], slot) * wide[slot // 4]).astype(BF16)
                weight[slot * HALF : (slot + 1) * HALF, z * 128 : (z + 1) * 128] = value
        columns = [cot[:, (z * Y + y) * 128 : (z * Y + y + 1) * 128] for z in range(Z_HI)]
        term = lax.dot_general(
            weight[...], jnp.concatenate(columns, axis=1), (((1,), (1,)), ((), ())), preferred_element_type=F32
        )
        if y == 0:
            total[...] = term
        else:
            total[...] += term
    for half in range(2):
        lanes = slice(half * 128, (half + 1) * 128)
        for slot in range(8):
            rows = pl.ds((slot // 4) * 4 * HALF + slot % 4, HALF, stride=4)
            ordered[half, rows, :] = total[slot * HALF : (slot + 1) * HALF, lanes]
        out_ref[lanes, :] = ordered[half].T.astype(BF16)


def grad_hidden_of(cot, blocks):
    rows = cot.shape[0]
    return pl.pallas_call(
        grad_hidden_kernel,
        in_specs=[pl.BlockSpec(memory_space=pl.ANY)] * 2,
        out_specs=pl.BlockSpec(memory_space=pltpu.VMEM),
        out_shape=jax.ShapeDtypeStruct((rows, HIDDEN_DEV), BF16),
        scratch_shapes=[
            pltpu.VMEM(cot.shape, BF16),
            pltpu.VMEM(blocks.shape, jnp.int32),
            pltpu.VMEM((HIDDEN_DEV, Z_HI * 128), BF16),
            pltpu.VMEM((HIDDEN_DEV, Z_HI * 128), BF16),
            pltpu.VMEM((HIDDEN_DEV, rows), F32),
            pltpu.VMEM((rows // 128, HIDDEN_DEV, 128), F32),
            pltpu.SemaphoreType.DMA((CHUNKS + 1,)),
        ],
        cost_estimate=pl.CostEstimate(
            flops=2 * rows * HIDDEN_DEV * cot.shape[1], bytes_accessed=6_000_000, transcendentals=0
        ),
        compiler_params=pltpu.CompilerParams(vmem_limit_bytes=VMEM_BYTES),
    )(cot, blocks)


def ring(size, step):
    return [(i, (i + step) % size) for i in range(size)]


def per_device(hidden, cotangent, packed_codes, block_scales):
    core, z_lo, x, z_hi = (lax.axis_index(name) for name in ("core", "z_lo", "x", "z_hi"))
    place = jnp.stack([core, z_lo, x % 2, z_hi]).astype(jnp.int32)

    hid = lax.all_gather(hidden, "y")
    near = lax.all_gather(pack_block(packed_codes, block_scales), "z_hi")

    first = ((z_lo * 2 + x % 2) * 2 + core) * SHARE
    mine = lax.dynamic_slice_in_dim(cotangent, first, SHARE, axis=0)
    mine = mine.reshape(SHARE, Z_HI, Y, 128).transpose(2, 0, 1, 3).reshape(Y, SHARE, Z_HI * 128)
    mine = lax.all_to_all(mine, "y", 0, 0)
    mine, near = lax.optimization_barrier((mine, near))
    parts = [mine]
    for flip_z, flip_x in ((1, 0), (0, 1), (1, 1)):
        pairs = [(z * X + i, (z ^ flip_z) * X + (i ^ flip_x)) for z in range(Z_LO) for i in range(X)]
        parts.append(lax.ppermute(mine, ("z_lo", "x"), pairs))
    weight = near_weight(near)
    weight, *parts = lax.optimization_barrier((weight, *parts))
    other = lax.ppermute(jnp.stack(parts), "core", ring(CORE, 1))
    cot = assemble(place, parts, other)
    hid, weight, cot = lax.optimization_barrier((hid, weight, cot))
    keep, send = ring_outputs(place, hid, weight)

    got = lax.ppermute(send, "core", ring(CORE, 1))
    hid, cot, send = lax.optimization_barrier((hid, cot, send))
    own, *others = gradient_terms(hid, cot)
    got, own, *others = lax.optimization_barrier((got, own, *others))
    pair = (keep.astype(F32) + got.astype(F32)).astype(BF16)

    pair, *others = lax.optimization_barrier((pair, *others))
    terms = [lax.ppermute(others[d - 1], "z_hi", ring(Z_HI, d)) for d in (2, 1, 3)]

    pieces = lax.all_to_all(pair, ("z_lo", "x"), 0, 0)
    rows = jnp.sum(pieces.astype(F32), axis=0).astype(BF16)
    output = lax.all_to_all(rows, "y", 0, 0)
    output = output.reshape(Y, 16, Z_HI, 128).transpose(1, 2, 0, 3).reshape(16, Z_HI * Y * 128)

    every = lax.all_gather(near, "y")
    every, rows = lax.optimization_barrier((every, rows))
    grad_hidden = grad_hidden_of(cotangent, every)
    grad_hidden, *terms = lax.optimization_barrier((grad_hidden, *terms))
    grad_weight = sum(term.astype(F32) for term in (own, *terms)).T
    return output, grad_hidden, grad_weight


def solution(mesh):
    fine = Mesh(mesh.devices.reshape(Z_LO, X, CORE, Z_HI, Y), FINE)
    inter, intra = ("z_lo", "x", "core"), ("z_hi", "y")
    return jax.shard_map(
        per_device,
        mesh=fine,
        in_specs=(P(intra, inter), P(intra, None), P(inter, intra), P(inter, intra)),
        out_specs=(P(intra + inter, None), P(intra, inter), P(inter, intra)),
        check_vma=False,
    )
```

```python
import functools

import jax
import jax.numpy as jnp
from jax import lax
from jax.experimental import pallas as pl
from jax.experimental.pallas import tpu as pltpu
from jax.sharding import Mesh, PartitionSpec as P

Z_LO, X, CORE, Z_HI, Y = 2, 4, 2, 4, 8
FINE = ("z_lo", "x", "core", "z_hi", "y")
BF16, F32 = jnp.bfloat16, jnp.float32
HALF = 112
HIDDEN_DEV = 896
SCALE_ROWS = 8
CHUNKS = 4
HALVES = 4
SHARE = 32
EXACT = 2.0**34
SIGNS = -0x77777778
VMEM_BYTES = 56 * 1024 * 1024
VMEM_PRODUCTS = 50 * 1024 * 1024


def pack_block(codes, scales):
    words = jnp.bitwise_or(codes[:HALF], jnp.left_shift(codes[HALF:], 16))
    words = jnp.bitwise_xor(words, SIGNS)
    whole = (scales * EXACT).astype(jnp.int32)
    whole = jnp.pad(whole, ((0, SCALE_ROWS - whole.shape[0]), (0, 0)))
    whole = jnp.broadcast_to(whole, (SCALE_ROWS, codes.shape[1]))
    return jnp.concatenate([words, whole], axis=0)


def level_of(words, slot):
    return jnp.right_shift(jnp.left_shift(words, 28 - 4 * slot), 28).astype(F32)


def scales_of(block):
    return block[HALF:].astype(F32) * (1.0 / EXACT)


def unpack_kernel(block_ref, out_ref, wide):
    block = block_ref[0]
    words, scales = block[:HALF], scales_of(block)
    for slot in range(8):
        wide[pl.ds((slot // 4) * 4 * HALF + slot % 4, HALF, stride=4), :] = level_of(words, slot)
    for b in range(HIDDEN_DEV // 128):
        rows = slice(b * 128, (b + 1) * 128)
        out_ref[rows, :] = (wide[rows, :] * scales[b : b + 1, :]).astype(BF16)


def near_weight(blocks):
    count, rows, lanes = blocks.shape
    return pl.pallas_call(
        unpack_kernel,
        grid=(count,),
        in_specs=[pl.BlockSpec((1, rows, lanes), lambda z: (z, 0, 0))],
        out_specs=pl.BlockSpec((HIDDEN_DEV, lanes), lambda z: (0, z)),
        out_shape=jax.ShapeDtypeStruct((HIDDEN_DEV, count * lanes), BF16),
        scratch_shapes=[pltpu.VMEM((HIDDEN_DEV, 128), F32)],
        cost_estimate=pl.CostEstimate(flops=2_000_000, bytes_accessed=1_200_000, transcendentals=0),
    )(blocks)


def assemble_kernel(place_ref, *refs):
    parts, other_ref, out_ref = refs[:4], refs[4], refs[5]
    core, z_lo, x_low, z_hi = place_ref[0], place_ref[1], place_ref[2], place_ref[3]
    order = [lax.rem(z_hi + d, Z_HI) for d in range(Z_HI)]
    for i in range(4):
        lo = z_lo if i % 2 == 0 else 1 - z_lo
        x = x_low if i // 2 == 0 else 1 - x_low
        for part, co in ((parts[i], core), (other_ref.at[i], 1 - core)):
            rows = pl.ds(pl.multiple_of(((lo * 2 + x) * 2 + co) * SHARE, SHARE), SHARE)
            for j, z in enumerate(order):
                out_ref[:, rows, j * 128 : (j + 1) * 128] = part[:, :, pl.ds(pl.multiple_of(z * 128, 128), 128)]


def assemble(place, parts, other):
    groups, share, width = parts[0].shape
    step = 4
    part = pl.BlockSpec((step, share, width), lambda g, place: (g, 0, 0))
    return pl.pallas_call(
        assemble_kernel,
        grid_spec=pltpu.PrefetchScalarGridSpec(
            num_scalar_prefetch=1,
            grid=(groups // step,),
            in_specs=[part] * 4 + [pl.BlockSpec((4, step, share, width), lambda g, place: (0, g, 0, 0))],
            out_specs=pl.BlockSpec((step, 8 * share, width), lambda g, place: (g, 0, 0)),
        ),
        out_shape=jax.ShapeDtypeStruct((groups, 8 * share, width), BF16),
        cost_estimate=pl.CostEstimate(flops=0, bytes_accessed=4_000_000, transcendentals=0),
        compiler_params=pltpu.CompilerParams(vmem_limit_bytes=VMEM_BYTES),
    )(place, *parts, other)


def outputs_kernel(place_ref, hid_ref, weight_ref, keep_ref, send_ref, hid, weight, keep, send, sems, out_sems):
    core = place_ref[0]
    groups, rows, depth = hid.shape
    step, width = groups // CHUNKS, weight.shape[1]
    load_weight = pltpu.make_async_copy(weight_ref, weight, sems.at[CHUNKS])
    loads = [
        pltpu.make_async_copy(hid_ref.at[pl.ds(i * step, step)], hid.at[pl.ds(i * step, step)], sems.at[i])
        for i in range(CHUNKS)
    ]
    load_weight.start()
    for load in loads:
        load.start()
    load_weight.wait()
    stores = []
    for i in range(CHUNKS):
        loads[i].wait()
        product = jnp.dot(
            hid[i * step : (i + 1) * step].reshape(step * rows, depth), weight[...], preferred_element_type=F32
        )
        product = product.astype(BF16).reshape(step, Z_LO * X, CORE, 16, width)
        for g in range(step):
            first, second = product[g, :, 0], product[g, :, 1]
            keep[:, i * step + g] = jnp.where(core == 0, first, second)
            send[:, i * step + g] = jnp.where(core == 0, second, first)
        at = pl.ds(i * step, step)
        stores.append(pltpu.make_async_copy(send.at[:, at], send_ref.at[:, at], out_sems.at[0, i]))
        stores.append(pltpu.make_async_copy(keep.at[:, at], keep_ref.at[:, at], out_sems.at[1, i]))
        for store in stores[-2:]:
            store.start()
    for store in stores:
        store.wait()


def ring_outputs(place, hid, weight):
    groups, _, depth = hid.shape
    width = weight.shape[1]
    part = (Z_LO * X, groups, 16, width)
    anywhere = pl.BlockSpec(memory_space=pl.ANY)
    return pl.pallas_call(
        outputs_kernel,
        grid_spec=pltpu.PrefetchScalarGridSpec(
            num_scalar_prefetch=1,
            grid=(1,),
            in_specs=[anywhere] * 2,
            out_specs=[anywhere] * 2,
            scratch_shapes=[
                pltpu.VMEM(hid.shape, BF16),
                pltpu.VMEM(weight.shape, BF16),
                pltpu.VMEM(part, BF16),
                pltpu.VMEM(part, BF16),
                pltpu.SemaphoreType.DMA((CHUNKS + 1,)),
                pltpu.SemaphoreType.DMA((2, CHUNKS)),
            ],
        ),
        out_shape=[jax.ShapeDtypeStruct(part, BF16)] * 2,
        cost_estimate=pl.CostEstimate(
            flops=2 * groups * 256 * depth * width, bytes_accessed=7_000_000, transcendentals=0
        ),
        compiler_params=pltpu.CompilerParams(vmem_limit_bytes=VMEM_PRODUCTS),
    )(place, hid, weight)


def terms_kernel(hid_ref, cot_ref, own_ref, up_ref, far_ref, down_ref, hid, cot, sems):
    groups, rows, depth = hid.shape
    step, width = groups // HALVES, cot.shape[2]
    loads = []
    for i in range(HALVES):
        at = pl.ds(i * step, step)
        loads.append(pltpu.make_async_copy(cot_ref.at[at], cot.at[at], sems.at[0, i]))
        loads.append(pltpu.make_async_copy(hid_ref.at[at], hid.at[at], sems.at[1, i]))
    for load in loads:
        load.start()
    total = None
    for i in range(HALVES):
        loads[2 * i].wait()
        loads[2 * i + 1].wait()
        part = slice(i * step, (i + 1) * step)
        term = lax.dot_general(
            cot[part].reshape(step * rows, width),
            hid[part].reshape(step * rows, depth),
            (((0,), (0,)), ((), ())),
            preferred_element_type=F32,
        )
        total = term if total is None else total + term
    for i, ref in enumerate((own_ref, up_ref, far_ref, down_ref)):
        ref[...] = total[i * 128 : (i + 1) * 128].astype(BF16)


def gradient_terms(hid, cot):
    groups, rows, depth = hid.shape
    width = cot.shape[2]
    return pl.pallas_call(
        terms_kernel,
        in_specs=[pl.BlockSpec(memory_space=pl.ANY)] * 2,
        out_specs=[pl.BlockSpec(memory_space=pltpu.VMEM)] * 4,
        scratch_shapes=[
            pltpu.VMEM(hid.shape, BF16),
            pltpu.VMEM(cot.shape, BF16),
            pltpu.SemaphoreType.DMA((2, HALVES)),
        ],
        out_shape=[jax.ShapeDtypeStruct((128, depth), BF16)] * 4,
        cost_estimate=pl.CostEstimate(
            flops=2 * groups * rows * depth * width, bytes_accessed=7_000_000, transcendentals=0
        ),
        compiler_params=pltpu.CompilerParams(vmem_limit_bytes=VMEM_PRODUCTS),
    )(hid, cot)


def row_widths(part):
    return ((0, 32), (1, 32), (2, 32), (3, 16)) if part == 0 else ((3, 16), (4, 32), (5, 32), (6, 32))


def grad_hidden_kernel(cot_ref, blocks_ref, out_ref, cot, blocks, even, odd, total, ordered, sems):
    step = Y // CHUNKS
    load_cot = pltpu.make_async_copy(cot_ref, cot, sems.at[CHUNKS])
    loads = [
        pltpu.make_async_copy(blocks_ref.at[pl.ds(i * step, step)], blocks.at[pl.ds(i * step, step)], sems.at[i])
        for i in range(CHUNKS)
    ]
    loads[0].start()
    load_cot.start()
    for load in loads[1:]:
        load.start()
    for y in range(Y):
        if y % step == 0:
            loads[y // step].wait()
        if y == 0:
            load_cot.wait()
        weight = odd if y % 2 else even
        for z in range(Z_HI):
            block = blocks[y, z]
            scales = scales_of(block)
            wide = [
                jnp.concatenate(
                    [jnp.broadcast_to(scales[b : b + 1], (rows, 128)) for b, rows in row_widths(part)], axis=0
                )
                for part in range(2)
            ]
            for slot in range(8):
                value = (level_of(block[:HALF], slot) * wide[slot // 4]).astype(BF16)
                weight[slot * HALF : (slot + 1) * HALF, z * 128 : (z + 1) * 128] = value
        columns = [cot[:, (z * Y + y) * 128 : (z * Y + y + 1) * 128] for z in range(Z_HI)]
        term = lax.dot_general(
            weight[...], jnp.concatenate(columns, axis=1), (((1,), (1,)), ((), ())), preferred_element_type=F32
        )
        if y == 0:
            total[...] = term
        else:
            total[...] += term
    for half in range(2):
        lanes = slice(half * 128, (half + 1) * 128)
        for slot in range(8):
            rows = pl.ds((slot // 4) * 4 * HALF + slot % 4, HALF, stride=4)
            ordered[half, rows, :] = total[slot * HALF : (slot + 1) * HALF, lanes]
        out_ref[lanes, :] = ordered[half].T.astype(BF16)


def grad_hidden_of(cot, blocks):
    rows = cot.shape[0]
    return pl.pallas_call(
        grad_hidden_kernel,
        in_specs=[pl.BlockSpec(memory_space=pl.ANY)] * 2,
        out_specs=pl.BlockSpec(memory_space=pltpu.VMEM),
        out_shape=jax.ShapeDtypeStruct((rows, HIDDEN_DEV), BF16),
        scratch_shapes=[
            pltpu.VMEM(cot.shape, BF16),
            pltpu.VMEM(blocks.shape, jnp.int32),
            pltpu.VMEM((HIDDEN_DEV, Z_HI * 128), BF16),
            pltpu.VMEM((HIDDEN_DEV, Z_HI * 128), BF16),
            pltpu.VMEM((HIDDEN_DEV, rows), F32),
            pltpu.VMEM((rows // 128, HIDDEN_DEV, 128), F32),
            pltpu.SemaphoreType.DMA((CHUNKS + 1,)),
        ],
        cost_estimate=pl.CostEstimate(
            flops=2 * rows * HIDDEN_DEV * cot.shape[1], bytes_accessed=6_000_000, transcendentals=0
        ),
        compiler_params=pltpu.CompilerParams(vmem_limit_bytes=VMEM_BYTES),
    )(cot, blocks)


def ring(size, step):
    return [(i, (i + step) % size) for i in range(size)]


def per_device(hidden, cotangent, packed_codes, block_scales):
    core, z_lo, x, z_hi = (lax.axis_index(name) for name in ("core", "z_lo", "x", "z_hi"))
    place = jnp.stack([core, z_lo, x % 2, z_hi]).astype(jnp.int32)

    hid = lax.all_gather(hidden, "y")
    near = lax.all_gather(pack_block(packed_codes, block_scales), "z_hi")

    first = ((z_lo * 2 + x % 2) * 2 + core) * SHARE
    mine = lax.dynamic_slice_in_dim(cotangent, first, SHARE, axis=0)
    mine = mine.reshape(SHARE, Z_HI, Y, 128).transpose(2, 0, 1, 3).reshape(Y, SHARE, Z_HI * 128)
    mine = lax.all_to_all(mine, "y", 0, 0)
    mine, near = lax.optimization_barrier((mine, near))
    parts = [mine]
    for flip_z, flip_x in ((1, 1), (1, 0), (0, 1)):
        pairs = [(z * X + i, (z ^ flip_z) * X + (i ^ flip_x)) for z in range(Z_LO) for i in range(X)]
        parts.append(lax.ppermute(mine, ("z_lo", "x"), pairs))
    parts.append(parts.pop(1))
    weight = near_weight(near)
    weight, *parts = lax.optimization_barrier((weight, *parts))
    other = lax.ppermute(jnp.stack(parts), "core", ring(CORE, 1))
    cot = assemble(place, parts, other)
    hid, weight, cot = lax.optimization_barrier((hid, weight, cot))
    keep, send = ring_outputs(place, hid, weight)

    got = lax.ppermute(send, "core", ring(CORE, 1))
    hid, cot, send = lax.optimization_barrier((hid, cot, send))
    own, *others = gradient_terms(hid, cot)
    got, own, *others = lax.optimization_barrier((got, own, *others))
    pair = (keep.astype(F32) + got.astype(F32)).astype(BF16)

    pair, *others = lax.optimization_barrier((pair, *others))
    terms = [lax.ppermute(others[d - 1], "z_hi", ring(Z_HI, d)) for d in (2, 1, 3)]

    pieces = lax.all_to_all(pair, ("z_lo", "x"), 0, 0)
    rows = jnp.sum(pieces.astype(F32), axis=0).astype(BF16)
    output = lax.all_to_all(rows, "y", 0, 0)
    output = output.reshape(Y, 16, Z_HI, 128).transpose(1, 2, 0, 3).reshape(16, Z_HI * Y * 128)

    every = lax.all_gather(near, "y")
    every, rows = lax.optimization_barrier((every, rows))
    grad_hidden = grad_hidden_of(cotangent, every)
    grad_hidden, *terms = lax.optimization_barrier((grad_hidden, *terms))
    grad_weight = sum(term.astype(F32) for term in (own, *terms)).T
    return output, grad_hidden, grad_weight


def solution(mesh):
    fine = Mesh(mesh.devices.reshape(Z_LO, X, CORE, Z_HI, Y), FINE)
    inter, intra = ("z_lo", "x", "core"), ("z_hi", "y")
    return jax.shard_map(
        per_device,
        mesh=fine,
        in_specs=(P(intra, inter), P(intra, None), P(inter, intra), P(inter, intra)),
        out_specs=(P(intra + inter, None), P(intra, inter), P(inter, intra)),
        check_vma=False,
    )
```
